32 devices in a mesh: dp: 8 (over z, x), et: 4 (over y, core).
Axes of the slice: x: 2, y: 2, z: 4, core: 2. Of those that a mesh axis runs over, the one named last changes fastest.
Arguments:
- tokens: bfloat16 [1024, 2048], P('dp', 'et'), may hold values from -6 to 6
- cotangent: bfloat16 [1024, 2048], P('dp', 'et'), may hold values from -1.5 to 1.5
- expert_ids: int32 [1024, 8], P('dp'), may hold values from 0 to 15, all different within a row; in each aligned block of 128 rows (0 to 127, 128 to 255, ...) at most 96 rows name the same one
- route_gates: bfloat16 [1024, 8], P('dp'), may hold values from 0.049804688 to 0.3984375
- gate_proj: bfloat16 [16, 2048, 1024], P('dp', None, 'et'), may hold values from -0.125 to 0.125
- up_proj: bfloat16 [16, 2048, 1024], P('dp', None, 'et'), may hold values from -0.125 to 0.125
- down_proj: bfloat16 [16, 1024, 2048], P('dp', 'et'), may hold values from -0.1875 to 0.1875
Outputs:
- mixed: bfloat16 [1024, 2048], P('dp', 'et')
- grad_tokens: bfloat16 [1024, 2048], P('dp', 'et')
- grad_gates: float32 [1024, 8], P('dp')
- grad_gate_proj: float32 [16, 2048, 1024], P('dp', None, 'et')
- grad_up_proj: float32 [16, 2048, 1024], P('dp', None, 'et')
- grad_down_proj: float32 [16, 1024, 2048], P('dp', 'et')
The draws below stay inside these ranges and needn't reach their ends.
Inputs may be any that keep to these rules, and one draw needn't show every extreme that they name: `expert_ids`: each row names 8 different experts. Among the rows of one device (128 aligned rows), no expert is named more than 96 times, a bound that some block reaches.
All inputs are finite; a program needn't handle non-finite values.
Results may differ from the reference program's by a relative error of at most 0.015.
Values may be sent and summed in bfloat16 or wider, within the bound.
A program may use at most 128 MiB of HBM per device.

```python
import math
import jax
import jax.numpy as jnp
import numpy as np
from jax import lax

D = 2048
FF = 1024
TOP = 8
TOK_DEV = 128
EXPERTS = 16
TOKENS = 1024
CAP = 96
UNITS = 256
N_ET = 4


def level_of(key, shape, cuts, least, top_value):
    factor_of = 1.0
    for dim, blocks in cuts:
        steps = jax.random.uniform(jax.random.fold_in(jax.random.fold_in(key, 6), dim), (blocks,), jnp.float32, least / len(cuts), top_value / len(cuts))
        factor_of = factor_of * jnp.repeat(jnp.exp(steps), shape[dim] // blocks).reshape((-1,) + (1,) * (len(shape) - 1 - dim))
    return factor_of


def shared_out(own_key, own, number, rows, number_of, top, bound, skew):
    sequence = jax.random.permutation(own_key, number_of)
    heavy_load, common = load_shares(number_of, rows * top, bound, skew, True), load_shares(number_of, rows * top, bound, skew, False)
    places = jnp.arange(number_of)

    def named(tallies, turn):
        used = int((tallies > 0).sum())
        fixed = max(1, used // 4)
        moved = fixed + (places - fixed + turn * (used - fixed)) % max(1, number_of - fixed)
        return jnp.zeros((number_of,), jnp.int32).at[sequence[jnp.where(places < fixed, places, moved)]].set(jnp.asarray(tallies, jnp.int32))

    tallies = jnp.where(number % 4 == 0, named(heavy_load, number // 4), named(common, number - number // 4 - 1))
    mixed = jax.random.permutation(jax.random.fold_in(own, 3), number_of)
    giver, sink = mixed[0:number_of // 2 * 2:2], mixed[1:number_of // 2 * 2:2]
    margin = jnp.minimum(tallies[giver] - 1, bound - tallies[sink]) // 2
    margin = jnp.where((giver == sequence[0]) | (sink == sequence[0]) | (tallies[sink] == 0), 0, jnp.maximum(margin, 0))
    moved = jax.random.randint(jax.random.fold_in(own, 4), (number_of // 2,), 0, 1 << 20) % (margin + 1)
    tallies = tallies.at[giver].add(-moved).at[sink].add(moved)
    items = jnp.searchsorted(jnp.cumsum(tallies), jnp.arange(rows * top), side="right").astype(jnp.int32)
    table = items.reshape(top, rows).T
    table = table[jax.random.permutation(jax.random.fold_in(own, 1), rows)]
    turn = jax.random.randint(jax.random.fold_in(own, 2), (rows, 1), 0, top)
    return jnp.take_along_axis(table, (jnp.arange(top)[None, :] + turn) % top, axis=1)


def load_shares(count, total, bound, skew, full):
    portions = [(1 << 20) // math.isqrt(standing ** skew) + 1 for standing in range(1, count + 1)]
    largest = bound if full else min(bound, max(-(-total // count), total * portions[0] // sum(portions)))
    least = 1 if total - largest >= count - 1 else 0
    counts, surplus = [largest] + [least] * (count - 1), total - largest - least * (count - 1)
    while surplus > 0:
        movable = [i for i in range(1, count) if counts[i] < largest] or [i for i in range(1, count) if counts[i] < bound]
        pool, left = sum([portions[i] for i in movable]), surplus
        for i in movable:
            extra = min(bound - counts[i], max(1, left * portions[i] // pool), surplus)
            counts[i] = counts[i] + extra
            surplus = surplus - extra
    return np.array(counts)


def scatter_about(key, shape, deviation, reach, shards=(), held_as=jnp.bfloat16):
    result = deviation * jax.random.normal(key, shape, jnp.float32)
    if shards:
        result = result * level_of(key, shape, shards, -0.22, 0.18)
    return jnp.clip(result, -reach, reach).astype(held_as)


def setup_inputs(seed: int = 0) -> dict:
    streams_of = jax.random.split(jax.random.key(seed), 8)
    tokens = scatter_about(streams_of[0], (TOKENS, D), 1.0, 6.0, ((0, 8), (1, 4)))
    cotangent = scatter_about(streams_of[1], (TOKENS, D), 0.25, 1.5, ((0, 8), (1, 4)))
    expert_ids_keys = jax.random.split(jax.random.fold_in(streams_of[2], 1), TOKENS // TOK_DEV)
    expert_ids_turns = jax.random.permutation(jax.random.fold_in(streams_of[2], 3), TOKENS // TOK_DEV)
    expert_ids = jax.vmap(lambda own, number: shared_out(jax.random.fold_in(streams_of[2], 2), own, number, TOK_DEV, EXPERTS, TOP, CAP, 2))(expert_ids_keys, expert_ids_turns).reshape((TOKENS, TOP))
    route_gates = jnp.clip(0.049804688 + 0.3486328 * jax.random.uniform(streams_of[3], (TOKENS, TOP), jnp.float32) ** level_of(streams_of[3], (TOKENS, TOP), ((0, 8),), -0.2, 0.2), 0.049804688, 0.3984375).astype(jnp.bfloat16)
    gate_proj = scatter_about(streams_of[4], (EXPERTS, D, FF), D ** -0.5, 0.125, ((0, 8), (2, 4)))
    up_proj = scatter_about(streams_of[5], (EXPERTS, D, FF), D ** -0.5, 0.125, ((0, 8), (2, 4)))
    down_proj = scatter_about(streams_of[6], (EXPERTS, FF, D), FF ** -0.5, 0.1875, ((0, 8), (1, 4)))
    return dict(tokens=tokens, cotangent=cotangent, expert_ids=expert_ids, route_gates=route_gates, gate_proj=gate_proj, up_proj=up_proj, down_proj=down_proj)


def places_in_block(chosen, experts):
    flattened = chosen.reshape(-1)
    onehot = (flattened[:, None] == jnp.arange(experts, dtype=jnp.int32)[None, :]).astype(jnp.int32)
    before = jnp.cumsum(onehot, axis=0) - onehot
    return jnp.sum(before * onehot, axis=1).astype(jnp.int32)


def reference(tokens, cotangent, expert_ids, route_gates, gate_proj, up_proj, down_proj):
    blocks = TOKENS // TOK_DEV
    assignments = TOKENS * TOP
    slot_span = blocks * CAP
    places = jax.vmap(lambda c: places_in_block(c, EXPERTS))(expert_ids.reshape(blocks, TOK_DEV, TOP)).reshape(-1)
    flattened = expert_ids.reshape(-1)
    source = (jnp.arange(assignments, dtype=jnp.int32) // (TOK_DEV * TOP)).astype(jnp.int32)
    slot_index = (flattened * slot_span + source * CAP + places).astype(jnp.int32)
    lookup = jnp.full((EXPERTS * slot_span,), assignments, jnp.int32).at[slot_index].set(jnp.arange(assignments, dtype=jnp.int32))
    lookup = lookup.reshape(EXPERTS, slot_span)
    tokens_ext = jnp.concatenate([tokens, jnp.zeros((1, D), jnp.bfloat16)], axis=0)
    cotangent_ext = jnp.concatenate([cotangent, jnp.zeros((1, D), jnp.bfloat16)], axis=0)
    gates_ext = jnp.concatenate([route_gates.reshape(-1).astype(jnp.float32), jnp.zeros((1,), jnp.float32)], axis=0)

    def per_expert(operands):
        rows_lookup, gate_matrix, up_matrix, down_matrix = operands
        holder = (rows_lookup // TOP).astype(jnp.int32)
        expert_in = tokens_ext[holder]
        expert_cot = (gates_ext[rows_lookup][:, None] * cotangent_ext[holder].astype(jnp.float32)).astype(jnp.bfloat16)
        pre_gate = jnp.dot(expert_in, gate_matrix, preferred_element_type=jnp.float32)
        pre_up = jnp.dot(expert_in, up_matrix, preferred_element_type=jnp.float32)
        sigmoid_gate = jax.nn.sigmoid(pre_gate)
        silu_gate = pre_gate * sigmoid_gate
        hidden = (silu_gate * pre_up).astype(jnp.bfloat16)
        hidden_groups = hidden.reshape(slot_span, N_ET, UNITS).astype(jnp.float32)
        down_groups = down_matrix.reshape(N_ET, UNITS, D).astype(jnp.float32)
        out_parts = jnp.einsum('sjf,jfd->jsd', hidden_groups, down_groups).astype(jnp.bfloat16)
        out_parts = lax.optimization_barrier(out_parts).astype(jnp.float32)
        expert_out = jnp.sum(out_parts, axis=0).astype(jnp.bfloat16)
        grad_hidden = jnp.dot(expert_cot, down_matrix.T, preferred_element_type=jnp.float32)
        grad_pre_gate = (grad_hidden * pre_up * sigmoid_gate * (1.0 + pre_gate * (1.0 - sigmoid_gate))).astype(jnp.bfloat16)
        grad_pre_up = (grad_hidden * silu_gate).astype(jnp.bfloat16)
        grad_down = jnp.dot(hidden.T, expert_cot, preferred_element_type=jnp.float32)
        grad_gate_w = jnp.dot(expert_in.T, grad_pre_gate, preferred_element_type=jnp.float32)
        grad_up_w = jnp.dot(expert_in.T, grad_pre_up, preferred_element_type=jnp.float32)
        gate_groups = gate_matrix.reshape(D, N_ET, UNITS).astype(jnp.float32)
        up_groups = up_matrix.reshape(D, N_ET, UNITS).astype(jnp.float32)
        in_parts = jnp.einsum('sjf,djf->jsd', grad_pre_gate.reshape(slot_span, N_ET, UNITS).astype(jnp.float32), gate_groups)
        in_parts = in_parts + jnp.einsum('sjf,djf->jsd', grad_pre_up.reshape(slot_span, N_ET, UNITS).astype(jnp.float32), up_groups)
        in_parts = lax.optimization_barrier(in_parts.astype(jnp.bfloat16)).astype(jnp.float32)
        grad_in = jnp.sum(in_parts, axis=0).astype(jnp.bfloat16)
        return expert_out, grad_in, grad_gate_w, grad_up_w, grad_down

    expert_out, grad_in, grad_gate_proj, grad_up_proj, grad_down_proj = lax.map(per_expert, (lookup, gate_proj, up_proj, down_proj))
    out_rows = expert_out.reshape(EXPERTS * slot_span, D)[slot_index].reshape(TOKENS, TOP, D).astype(jnp.float32)
    grad_rows = grad_in.reshape(EXPERTS * slot_span, D)[slot_index].reshape(TOKENS, TOP, D).astype(jnp.float32)
    mixed = jnp.sum(route_gates.astype(jnp.float32)[:, :, None] * out_rows, axis=1).astype(jnp.bfloat16)
    grad_gates = jnp.sum(cotangent.astype(jnp.float32)[:, None, :] * out_rows, axis=2)
    grad_tokens = jnp.sum(grad_rows, axis=1).astype(jnp.bfloat16)
    return mixed, grad_tokens, grad_gates, grad_gate_proj, grad_up_proj, grad_down_proj
```

```python
import jax
import jax.numpy as jnp
from jax import lax
from jax.sharding import PartitionSpec as P

F32 = jnp.float32
BF16 = jnp.bfloat16


def dot(a, b, ca, cb):
    return lax.dot_general(a, b, (((ca,), (cb,)), ((), ())), preferred_element_type=F32)


def piece(tokens, cotangent, expert_ids, route_gates, gate_proj, up_proj, down_proj):
    groups = lax.axis_size("dp")
    parts = lax.axis_size("et")
    mine, features, units = gate_proj.shape
    experts = mine * groups
    rows, width = tokens.shape
    total = rows * groups
    chosen = expert_ids[:, :, None] == jnp.arange(experts, dtype=jnp.int32)
    weight = jnp.sum(jnp.where(chosen, route_gates.astype(F32)[:, :, None], 0.0), axis=1)
    weights = lax.all_to_all(
        weight.reshape(rows, groups, mine).transpose(1, 0, 2), "dp", 0, 0, tiled=True
    ).reshape(total, mine)
    x = lax.all_gather(lax.all_gather(tokens, "dp", axis=0, tiled=True), "et", axis=1, tiled=True)
    c = lax.all_gather(lax.all_gather(cotangent, "dp", axis=0, tiled=True), "et", axis=1, tiled=True)
    weighted, pre_grads, inner = [], [], []
    for e in range(mine):
        g = weights[:, e : e + 1]
        pre_gate = dot(x, gate_proj[e], 1, 0)
        pre_up = dot(x, up_proj[e], 1, 0)
        back = dot(c, down_proj[e], 1, 1)
        s = jax.nn.sigmoid(pre_gate)
        silu = pre_gate * s
        hidden = silu * pre_up
        grad = back * g
        weighted.append((hidden * g).astype(BF16))
        pre_grads.append((grad * pre_up * s * (1.0 + pre_gate * (1.0 - s))).astype(BF16))
        pre_grads.append((grad * silu).astype(BF16))
        inner.append(jnp.sum(hidden * back, axis=1))
    out_part = sum(dot(weighted[e], down_proj[e], 1, 0) for e in range(mine)).astype(BF16)
    in_part = sum(
        dot(pre_grads[2 * e], gate_proj[e], 1, 1) + dot(pre_grads[2 * e + 1], up_proj[e], 1, 1)
        for e in range(mine)
    ).astype(BF16)
    sums = [
        lax.psum_scatter(
            lax.psum_scatter(part, "et", scatter_dimension=1, tiled=True),
            "dp",
            scatter_dimension=0,
            tiled=True,
        )
        for part in (out_part, in_part)
    ]
    grad_down = jnp.stack([dot(weighted[e], c, 0, 0) for e in range(mine)])
    grad_gate_w = jnp.stack([dot(x, pre_grads[2 * e], 0, 0) for e in range(mine)])
    grad_up_w = jnp.stack([dot(x, pre_grads[2 * e + 1], 0, 0) for e in range(mine)])
    inner = lax.psum(jnp.stack(inner, 1), "et").reshape(groups, rows, mine)
    inner = lax.all_to_all(inner, "dp", 0, 0, tiled=True).transpose(1, 0, 2).reshape(rows, experts)
    grad_gates = jnp.sum(jnp.where(chosen, inner[:, None, :], 0.0), axis=2)
    return (sums[0], sums[1], grad_gates, grad_gate_w, grad_up_w, grad_down)


def local(tokens, cotangent, expert_ids, route_gates, gate_proj, up_proj, down_proj):
    rows = tokens.shape[0]
    pieces = max(1, rows * lax.axis_size("dp") // 1024)
    held = (gate_proj, up_proj, down_proj)
    if pieces == 1 or rows % (16 * pieces):
        return piece(tokens, cotangent, expert_ids, route_gates, *held)

    def step(grads, part):
        done = piece(*part, *held)
        return tuple(a + b for a, b in zip(grads, done[3:])), done[:3]

    split = lambda a: a.reshape(pieces, rows // pieces, *a.shape[1:])
    grads, done = lax.scan(
        step,
        tuple(jnp.zeros(a.shape, F32) for a in held),
        tuple(split(a) for a in (tokens, cotangent, expert_ids, route_gates)),
    )
    return tuple(a.reshape(rows, *a.shape[2:]) for a in done) + grads


def solution(mesh):
    in_specs = (
        P("dp", "et"),
        P("dp", "et"),
        P("dp", None),
        P("dp", None),
        P("dp", None, "et"),
        P("dp", None, "et"),
        P("dp", "et", None),
    )
    out_specs = (
        P("dp", "et"),
        P("dp", "et"),
        P("dp", None),
        P("dp", None, "et"),
        P("dp", None, "et"),
        P("dp", "et", None),
    )
    return jax.shard_map(local, mesh=mesh, in_specs=in_specs, out_specs=out_specs, check_vma=False)
```

```python
import functools
import itertools
import jax
import jax.numpy as jnp
from jax import lax
from jax.experimental import pallas as pl
from jax.experimental.pallas import tpu as pltpu
from jax.sharding import PartitionSpec as P

F32 = jnp.float32
BF16 = jnp.bfloat16


def sizes():
    groups, parts = lax.axis_size("dp"), lax.axis_size("et")
    across = 2 if groups <= 8 else 4
    return {"z": groups // across, "x": across, "y": parts // 2, "c": 2}


def position(size):
    dp, et = lax.axis_index("dp"), lax.axis_index("et")
    return {"z": dp // size["x"], "x": dp % size["x"], "y": et // 2, "c": et % 2}


def device(size, at):
    return (at["z"] * size["x"] + at["x"], at["y"] * 2 + at["c"])


def beside(size, at, axis, step):
    return {**at, axis: lax.rem(at[axis] + step, size[axis])}


def greet(size, me):
    barrier = pltpu.get_barrier_semaphore()
    count = 0
    for axis in size:
        for step in range(1, size[axis]):
            pl.semaphore_signal(
                barrier,
                inc=1,
                device_id=device(size, beside(size, me, axis, step)),
                device_id_type=pl.DeviceIdType.MESH,
            )
            count += 1
    pl.semaphore_wait(barrier, count)


def block(ref, size, at):
    rows, width = (ref.shape[0] // (size["z"] * size["x"]), ref.shape[1] // (size["y"] * 2))
    dp, et = device(size, at)
    return ref.at[
        pl.ds(pl.multiple_of(dp * rows, rows), rows),
        pl.ds(pl.multiple_of(et * width, width), width),
    ]


ORDERS = (("z", "x", "y", "c"), ("z", "y", "x", "c"))


def gather_kernel(size, t_ref, c_ref, w_ref, x_out, c_out, w_out, own, sends, recvs):
    me = position(size)
    greet(size, me)
    sources = (t_ref, c_ref, w_ref)
    targets = (x_out, c_out, w_out)
    orders = ORDERS + (("z", "x"),)

    def place(t, at):
        if t < 2:
            return block(targets[t], size, at)
        rows = w_ref.shape[0]
        dp = device(size, at)[0]
        return w_out.at[pl.ds(pl.multiple_of(dp * rows, rows), rows), :]

    def index(at):
        dp, et = device(size, at)
        return dp * (size["y"] * 2) + et

    started = []

    def forward(t, at, source, stage):
        for axis in orders[t][stage:]:
            for step in range(1, size[axis]):
                copy = pltpu.make_async_remote_copy(
                    src_ref=source,
                    dst_ref=place(t, at),
                    send_sem=sends.at[len(started)],
                    recv_sem=recvs.at[t, index(at)],
                    device_id=device(size, beside(size, me, axis, step)),
                    device_id_type=pl.DeviceIdType.MESH,
                )
                copy.start()
                started.append(copy)

    for t in (2, 0, 1):
        forward(t, me, sources[t], 0)
    kept = []
    for t in range(3):
        copy = pltpu.make_async_copy(sources[t], place(t, me), own.at[t])
        copy.start()
        kept.append(copy)
    for stage in range(4):
        lists = []
        for t in (2, 0, 1):
            order = orders[t]
            if stage >= len(order):
                continue
            axis = order[stage]
            steps = [range(size[a]) for a in order[:stage]] + [range(1, size[axis])]
            lists.append([(t, tuple(zip(order, walk))) for walk in itertools.product(*steps)])
        for group in itertools.zip_longest(*lists):
            for item in group:
                if item is None:
                    continue
                t, walk = item
                at = dict(me)
                for axis, step in walk:
                    at = beside(size, at, axis, step) if step else at
                pltpu.make_async_copy(place(t, at), place(t, at), recvs.at[t, index(at)]).wait()
                forward(t, at, place(t, at), stage + 1)
    for copy in kept:
        copy.wait()
    for copy in started:
        copy.wait_send()


def gather(tokens, cotangent, weight):
    size = sizes()
    groups, parts = size["z"] * size["x"], size["y"] * 2
    rows, width = tokens.shape
    whole = jax.ShapeDtypeStruct((rows * groups, width * parts), BF16)
    anywhere = pl.BlockSpec(memory_space=pl.ANY)
    copies = 2 * (groups * parts - 1) + groups - 1
    return pl.pallas_call(
        functools.partial(gather_kernel, size),
        out_shape=(whole, whole, jax.ShapeDtypeStruct((rows * groups, weight.shape[1]), BF16)),
        in_specs=[anywhere] * 3,
        out_specs=[anywhere] * 3,
        scratch_shapes=[
            pltpu.SemaphoreType.DMA((3,)),
            pltpu.SemaphoreType.DMA((copies,)),
            pltpu.SemaphoreType.DMA((3, groups * parts)),
        ],
        compiler_params=pltpu.CompilerParams(collective_id=0, has_side_effects=True),
        name="gather",
    )(tokens, cotangent, weight)


def scatter_kernel(size, m_ref, g_ref, m_out, g_out, first, second0, second1, third0, third1,
                   last, sends, r0, r1, r2, r3):
    me = position(size)
    greet(size, me)
    parts = (m_ref, g_ref)
    outs = (m_out, g_out)
    seconds, thirds = (second0, second1), (third0, third1)
    orders = (("y", "x"), ("x", "y"))
    started = []

    def send(source, target, recv, axis, step):
        copy = pltpu.make_async_remote_copy(
            src_ref=source,
            dst_ref=target,
            send_sem=sends.at[len(started)],
            recv_sem=recv,
            device_id=device(size, beside(size, me, axis, step)),
            device_id_type=pl.DeviceIdType.MESH,
        )
        copy.start()
        started.append(copy)

    def arrived(ref, sem):
        pltpu.make_async_copy(ref, ref, sem).wait()

    def along(t, a, b, k):
        at = dict(me)
        for axis, step in zip(orders[t] + ("z",), (a, b, k)):
            at = beside(size, at, axis, step) if step else at
        return at

    walks = []
    for t in range(2):
        na, nb = (size[axis] for axis in orders[t])
        walks.append(
            [(a, b, k) for a in reversed(range(na)) for b in reversed(range(nb))
             for k in reversed(range(size["z"]))]
        )
    for walk0, walk1 in zip(*walks):
        for t, walk in ((0, walk0), (1, walk1)):
            n = walks[t].index(walk)
            to = beside(size, along(t, *walk), "c", 1)
            send(block(parts[t], size, to), first.at[t, n], r0.at[t, n], "c", 1)
    for i in range(len(walks[0])):
        for t in range(2):
            a, b, k = walks[t][i]
            arrived(first.at[t, i], r0.at[t, i])
            own = block(parts[t], size, along(t, a, b, k))
            first[t, i] = (first[t, i].astype(F32) + own[...].astype(F32)).astype(BF16)
            if a:
                slot = b * size["z"] + k
                send(first.at[t, i], seconds[t].at[a - 1, slot], r1.at[t, a - 1, slot], orders[t][0], a)
    pairs = [
        [(b, k) for b in reversed(range(size[orders[t][1]])) for k in reversed(range(size["z"]))]
        for t in range(2)
    ]
    for i in range(len(pairs[0])):
        for t in range(2):
            b, k = pairs[t][i]
            slot = b * size["z"] + k
            n = walks[t].index((0, b, k))
            total = first[t, n].astype(F32)
            for d in range(size[orders[t][0]] - 1):
                arrived(seconds[t].at[d, slot], r1.at[t, d, slot])
                total = total + seconds[t][d, slot].astype(F32)
            seconds[t][0, slot] = total.astype(BF16)
            if b:
                send(seconds[t].at[0, slot], thirds[t].at[b - 1, k], r2.at[t, b - 1, k], orders[t][1], b)
    for k in reversed(range(size["z"])):
        for t in range(2):
            total = seconds[t][0, k].astype(F32)
            for d in range(size[orders[t][1]] - 1):
                arrived(thirds[t].at[d, k], r2.at[t, d, k])
                total = total + thirds[t][d, k].astype(F32)
            thirds[t][0, k] = total.astype(BF16)
            if k:
                send(thirds[t].at[0, k], last.at[t, k - 1], r3.at[t, k - 1], "z", k)
    for t in range(2):
        total = thirds[t][0, 0].astype(F32)
        for d in range(size["z"] - 1):
            arrived(last.at[t, d], r3.at[t, d])
            total = total + last[t, d].astype(F32)
        outs[t][...] = total.astype(BF16)
    for copy in started:
        copy.wait_send()


def scatter(out_part, in_part):
    size = sizes()
    nz, nx, ny = size["z"], size["x"], size["y"]
    rows, width = out_part.shape[0] // (nz * nx), out_part.shape[1] // (ny * 2)
    one = jax.ShapeDtypeStruct((rows, width), BF16)
    inside = pl.BlockSpec(memory_space=pltpu.VMEM)
    dma = pltpu.SemaphoreType.DMA
    wide = max(nx, ny)
    return pl.pallas_call(
        functools.partial(scatter_kernel, size),
        out_shape=(one, one),
        in_specs=[inside] * 2,
        out_specs=[inside] * 2,
        scratch_shapes=[
            pltpu.VMEM((2, nz * nx * ny, rows, width), BF16),
            pltpu.VMEM((ny - 1, nx * nz, rows, width), BF16),
            pltpu.VMEM((nx - 1, ny * nz, rows, width), BF16),
            pltpu.VMEM((nx - 1, nz, rows, width), BF16),
            pltpu.VMEM((ny - 1, nz, rows, width), BF16),
            pltpu.VMEM((2, nz - 1, rows, width), BF16),
            dma((4 * nz * nx * ny + 2 * nz,)),
            dma((2, nz * nx * ny)),
            dma((2, wide - 1, wide * nz)),
            dma((2, wide - 1, nz)),
            dma((2, nz - 1)),
        ],
        compiler_params=pltpu.CompilerParams(
            collective_id=1, has_side_effects=True, vmem_limit_bytes=40 * 2**20
        ),
        name="scatter",
    )(out_part, in_part)


def dot(a, b, ca, cb):
    return lax.dot_general(a, b, (((ca,), (cb,)), ((), ())), preferred_element_type=F32)


def piece(tokens, cotangent, expert_ids, route_gates, gate_proj, up_proj, down_proj):
    groups = lax.axis_size("dp")
    mine, features, units = gate_proj.shape
    experts = mine * groups
    rows, width = tokens.shape
    total = rows * groups
    chosen = expert_ids[:, :, None] == jnp.arange(experts, dtype=jnp.int32)
    weight = jnp.sum(jnp.where(chosen, route_gates.astype(F32)[:, :, None], 0.0), axis=1)
    lanes = -experts % 128
    x, c, weights = gather(tokens, cotangent, jnp.pad(weight, ((0, 0), (0, lanes))).astype(BF16))
    weights = lax.dynamic_slice_in_dim(weights, lax.axis_index("dp") * mine, mine, 1).astype(F32)
    weighted, pre_grads, inner = [], [], []
    for e in range(mine):
        g = weights[:, e : e + 1]
        pre_gate = dot(x, gate_proj[e], 1, 0)
        pre_up = dot(x, up_proj[e], 1, 0)
        back = dot(c, down_proj[e], 1, 1)
        s = jax.nn.sigmoid(pre_gate)
        silu = pre_gate * s
        hidden = silu * pre_up
        grad = back * g
        weighted.append((hidden * g).astype(BF16))
        pre_grads.append((grad * pre_up * s * (1.0 + pre_gate * (1.0 - s))).astype(BF16))
        pre_grads.append((grad * silu).astype(BF16))
        inner.append(jnp.sum(hidden * back, axis=1))
    out_part = sum(dot(weighted[e], down_proj[e], 1, 0) for e in range(mine)).astype(BF16)
    in_part = sum(
        dot(pre_grads[2 * e], gate_proj[e], 1, 1) + dot(pre_grads[2 * e + 1], up_proj[e], 1, 1)
        for e in range(mine)
    ).astype(BF16)
    sums = lax.optimization_barrier(scatter(out_part, in_part))
    grad_down = jnp.stack([dot(weighted[e], c, 0, 0) for e in range(mine)])
    grad_gate_w = jnp.stack([dot(x, pre_grads[2 * e], 0, 0) for e in range(mine)])
    grad_up_w = jnp.stack([dot(x, pre_grads[2 * e + 1], 0, 0) for e in range(mine)])
    inner = lax.psum(jnp.stack(inner, 1), "et").reshape(groups, rows, mine)
    inner = lax.all_to_all(inner, "dp", 0, 0, tiled=True).transpose(1, 0, 2).reshape(rows, experts)
    grad_gates = jnp.sum(jnp.where(chosen, inner[:, None, :], 0.0), axis=2)
    return (sums[0], sums[1], grad_gates, grad_gate_w, grad_up_w, grad_down)


def local(tokens, cotangent, expert_ids, route_gates, gate_proj, up_proj, down_proj):
    rows = tokens.shape[0]
    pieces = max(1, rows * lax.axis_size("dp") // 1024)
    held = (gate_proj, up_proj, down_proj)
    if pieces == 1 or rows % (16 * pieces):
        return piece(tokens, cotangent, expert_ids, route_gates, *held)

    def step(grads, part):
        done = piece(*part, *held)
        return tuple(a + b for a, b in zip(grads, done[3:])), done[:3]

    split = lambda a: a.reshape(pieces, rows // pieces, *a.shape[1:])
    grads, done = lax.scan(
        step,
        tuple(jnp.zeros(a.shape, F32) for a in held),
        tuple(split(a) for a in (tokens, cotangent, expert_ids, route_gates)),
    )
    return tuple(a.reshape(rows, *a.shape[2:]) for a in done) + grads


def solution(mesh):
    in_specs = (
        P("dp", "et"),
        P("dp", "et"),
        P("dp", None),
        P("dp", None),
        P("dp", None, "et"),
        P("dp", None, "et"),
        P("dp", "et", None),
    )
    out_specs = (
        P("dp", "et"),
        P("dp", "et"),
        P("dp", None),
        P("dp", None, "et"),
        P("dp", None, "et"),
        P("dp", "et", None),
    )
    return jax.shard_map(local, mesh=mesh, in_specs=in_specs, out_specs=out_specs, check_vma=False)
```

```python
import functools
import itertools
import jax
import jax.numpy as jnp
from jax import lax
from jax.experimental import pallas as pl
from jax.experimental.pallas import tpu as pltpu
from jax.sharding import PartitionSpec as P

F32 = jnp.float32
BF16 = jnp.bfloat16


def sizes():
    groups, parts = lax.axis_size("dp"), lax.axis_size("et")
    across = 2 if groups <= 8 else 4
    return {"z": groups // across, "x": across, "y": parts // 2, "c": 2}


def position(size):
    dp, et = lax.axis_index("dp"), lax.axis_index("et")
    return {"z": dp // size["x"], "x": dp % size["x"], "y": et // 2, "c": et % 2}


def device(size, at):
    return (at["z"] * size["x"] + at["x"], at["y"] * 2 + at["c"])


def beside(size, at, axis, step):
    return {**at, axis: lax.rem(at[axis] + step, size[axis])}


def greet(size, me):
    barrier = pltpu.get_barrier_semaphore()
    count = 0
    for axis in size:
        for step in range(1, size[axis]):
            pl.semaphore_signal(
                barrier,
                inc=1,
                device_id=device(size, beside(size, me, axis, step)),
                device_id_type=pl.DeviceIdType.MESH,
            )
            count += 1
    pl.semaphore_wait(barrier, count)


def block(ref, size, at):
    rows, width = (ref.shape[0] // (size["z"] * size["x"]), ref.shape[1] // (size["y"] * 2))
    dp, et = device(size, at)
    return ref.at[
        pl.ds(pl.multiple_of(dp * rows, rows), rows),
        pl.ds(pl.multiple_of(et * width, width), width),
    ]


ORDERS = (("z", "x", "y", "c"), ("z", "y", "x", "c"))


def gather_kernel(size, t_ref, c_ref, w_ref, x_out, c_out, w_out, own, sends, recvs):
    me = position(size)
    greet(size, me)
    sources = (t_ref, c_ref, w_ref)
    targets = (x_out, c_out, w_out)
    orders = ORDERS + (("z", "x"),)

    def place(t, at):
        if t < 2:
            return block(targets[t], size, at)
        rows = w_ref.shape[0]
        dp = device(size, at)[0]
        return w_out.at[pl.ds(pl.multiple_of(dp * rows, rows), rows), :]

    def index(at):
        dp, et = device(size, at)
        return dp * (size["y"] * 2) + et

    started = []

    def forward(t, at, source, stage):
        for axis in orders[t][stage:]:
            for step in range(1, size[axis]):
                copy = pltpu.make_async_remote_copy(
                    src_ref=source,
                    dst_ref=place(t, at),
                    send_sem=sends.at[len(started)],
                    recv_sem=recvs.at[t, index(at)],
                    device_id=device(size, beside(size, me, axis, step)),
                    device_id_type=pl.DeviceIdType.MESH,
                )
                copy.start()
                started.append(copy)

    for t in (2, 0, 1):
        forward(t, me, sources[t], 0)
    kept = []
    for t in range(3):
        copy = pltpu.make_async_copy(sources[t], place(t, me), own.at[t])
        copy.start()
        kept.append(copy)
    for stage in range(4):
        lists = []
        for t in (2, 0, 1):
            order = orders[t]
            if stage >= len(order):
                continue
            axis = order[stage]
            steps = [range(size[a]) for a in order[:stage]] + [range(1, size[axis])]
            lists.append([(t, tuple(zip(order, walk))) for walk in itertools.product(*steps)])
        for group in itertools.zip_longest(*lists):
            for item in group:
                if item is None:
                    continue
                t, walk = item
                at = dict(me)
                for axis, step in walk:
                    at = beside(size, at, axis, step) if step else at
                pltpu.make_async_copy(place(t, at), place(t, at), recvs.at[t, index(at)]).wait()
                forward(t, at, place(t, at), stage + 1)
    for copy in kept:
        copy.wait()
    for copy in started:
        copy.wait_send()


def gather(tokens, cotangent, weight):
    size = sizes()
    groups, parts = size["z"] * size["x"], size["y"] * 2
    rows, width = tokens.shape
    whole = jax.ShapeDtypeStruct((rows * groups, width * parts), BF16)
    anywhere = pl.BlockSpec(memory_space=pl.ANY)
    copies = 2 * (groups * parts - 1) + groups - 1
    return pl.pallas_call(
        functools.partial(gather_kernel, size),
        out_shape=(whole, whole, jax.ShapeDtypeStruct((rows * groups, weight.shape[1]), BF16)),
        in_specs=[anywhere] * 3,
        out_specs=[anywhere] * 3,
        scratch_shapes=[
            pltpu.SemaphoreType.DMA((3,)),
            pltpu.SemaphoreType.DMA((copies,)),
            pltpu.SemaphoreType.DMA((3, groups * parts)),
        ],
        compiler_params=pltpu.CompilerParams(collective_id=0, has_side_effects=True),
        name="gather",
    )(tokens, cotangent, weight)


def scatter_kernel(size, m_ref, g_ref, m_out, g_out, first, second0, second1, third0, third1,
                   last, sends, r0, r1, r2, r3):
    me = position(size)
    greet(size, me)
    parts = (m_ref, g_ref)
    outs = (m_out, g_out)
    seconds, thirds = (second0, second1), (third0, third1)
    orders = (("y", "x"), ("x", "y"))
    started = []

    def send(source, target, recv, axis, step):
        copy = pltpu.make_async_remote_copy(
            src_ref=source,
            dst_ref=target,
            send_sem=sends.at[len(started)],
            recv_sem=recv,
            device_id=device(size, beside(size, me, axis, step)),
            device_id_type=pl.DeviceIdType.MESH,
        )
        copy.start()
        started.append(copy)

    def arrived(ref, sem):
        pltpu.make_async_copy(ref, ref, sem).wait()

    def along(t, a, b, k):
        at = dict(me)
        for axis, step in zip(orders[t] + ("z",), (a, b, k)):
            at = beside(size, at, axis, step) if step else at
        return at

    walks = []
    for t in range(2):
        na, nb = (size[axis] for axis in orders[t])
        walks.append(
            [(a, b, k) for a in reversed(range(na)) for b in reversed(range(nb))
             for k in reversed(range(size["z"]))]
        )
    for walk0, walk1 in zip(*walks):
        for t, walk in ((0, walk0), (1, walk1)):
            n = walks[t].index(walk)
            to = beside(size, along(t, *walk), "c", 1)
            send(block(parts[t], size, to), first.at[t, n], r0.at[t, n], "c", 1)
    for i in range(len(walks[0])):
        for t in range(2):
            a, b, k = walks[t][i]
            arrived(first.at[t, i], r0.at[t, i])
            own = block(parts[t], size, along(t, a, b, k))
            first[t, i] = (first[t, i].astype(F32) + own[...].astype(F32)).astype(BF16)
            if a:
                slot = b * size["z"] + k
                send(first.at[t, i], seconds[t].at[a - 1, slot], r1.at[t, a - 1, slot], orders[t][0], a)
    pairs = [
        [(b, k) for b in reversed(range(size[orders[t][1]])) for k in reversed(range(size["z"]))]
        for t in range(2)
    ]
    for i in range(len(pairs[0])):
        for t in range(2):
            b, k = pairs[t][i]
            slot = b * size["z"] + k
            n = walks[t].index((0, b, k))
            total = first[t, n].astype(F32)
            for d in range(size[orders[t][0]] - 1):
                arrived(seconds[t].at[d, slot], r1.at[t, d, slot])
                total = total + seconds[t][d, slot].astype(F32)
            seconds[t][0, slot] = total.astype(BF16)
            if b:
                send(seconds[t].at[0, slot], thirds[t].at[b - 1, k], r2.at[t, b - 1, k], orders[t][1], b)
    for k in reversed(range(size["z"])):
        for t in range(2):
            total = seconds[t][0, k].astype(F32)
            for d in range(size[orders[t][1]] - 1):
                arrived(thirds[t].at[d, k], r2.at[t, d, k])
                total = total + thirds[t][d, k].astype(F32)
            thirds[t][0, k] = total.astype(BF16)
            if k:
                send(thirds[t].at[0, k], last.at[t, k - 1], r3.at[t, k - 1], "z", k)
    for t in range(2):
        total = thirds[t][0, 0].astype(F32)
        for d in range(size["z"] - 1):
            arrived(last.at[t, d], r3.at[t, d])
            total = total + last[t, d].astype(F32)
        outs[t][...] = total.astype(BF16)
    for copy in started:
        copy.wait_send()


def scatter(out_part, in_part):
    size = sizes()
    nz, nx, ny = size["z"], size["x"], size["y"]
    rows, width = out_part.shape[0] // (nz * nx), out_part.shape[1] // (ny * 2)
    one = jax.ShapeDtypeStruct((rows, width), BF16)
    inside = pl.BlockSpec(memory_space=pltpu.VMEM)
    dma = pltpu.SemaphoreType.DMA
    wide = max(nx, ny)
    return pl.pallas_call(
        functools.partial(scatter_kernel, size),
        out_shape=(one, one),
        in_specs=[inside] * 2,
        out_specs=[inside] * 2,
        scratch_shapes=[
            pltpu.VMEM((2, nz * nx * ny, rows, width), BF16),
            pltpu.VMEM((ny - 1, nx * nz, rows, width), BF16),
            pltpu.VMEM((nx - 1, ny * nz, rows, width), BF16),
            pltpu.VMEM((nx - 1, nz, rows, width), BF16),
            pltpu.VMEM((ny - 1, nz, rows, width), BF16),
            pltpu.VMEM((2, nz - 1, rows, width), BF16),
            dma((4 * nz * nx * ny + 2 * nz,)),
            dma((2, nz * nx * ny)),
            dma((2, wide - 1, wide * nz)),
            dma((2, wide - 1, nz)),
            dma((2, nz - 1)),
        ],
        compiler_params=pltpu.CompilerParams(
            collective_id=1, has_side_effects=True, vmem_limit_bytes=40 * 2**20
        ),
        name="scatter",
    )(out_part, in_part)


def dot(a, b, ca, cb):
    return lax.dot_general(a, b, (((ca,), (cb,)), ((), ())), preferred_element_type=F32)


def grads_kernel(mine, x_ref, c_ref, *refs):
    gate_out, up_out, down_out = refs[3 * mine :]
    x, c = x_ref[...], c_ref[...]
    for e in range(mine):
        hidden, gate, up = (ref[...] for ref in refs[3 * e : 3 * e + 3])
        gate_out[e] = dot(x, gate, 0, 0)
        up_out[e] = dot(x, up, 0, 0)
        down_out[e] = dot(hidden, c, 0, 0)


def weight_grads(x, c, weighted, pre_grads):
    mine, (total, features), units = len(weighted), x.shape, weighted[0].shape[1]
    width = 512
    columns = pl.BlockSpec((total, width), lambda j: (0, j))
    tall = pl.BlockSpec((mine, width, units), lambda j: (0, j, 0))
    flat = [a for e in range(mine) for a in (weighted[e], pre_grads[2 * e], pre_grads[2 * e + 1])]
    return pl.pallas_call(
        functools.partial(grads_kernel, mine),
        grid=(features // width,),
        out_shape=(
            jax.ShapeDtypeStruct((mine, features, units), F32),
            jax.ShapeDtypeStruct((mine, features, units), F32),
            jax.ShapeDtypeStruct((mine, units, features), F32),
        ),
        in_specs=[columns, columns]
        + [pl.BlockSpec((total, units), lambda j: (0, 0)) for _ in flat],
        out_specs=[tall, tall, pl.BlockSpec((mine, units, width), lambda j: (0, 0, j))],
        compiler_params=pltpu.CompilerParams(vmem_limit_bytes=40 * 2**20),
        cost_estimate=pl.CostEstimate(
            flops=6 * mine * total * features * units,
            bytes_accessed=4 * total * features + 12 * mine * features * units,
            transcendentals=0,
        ),
        name="weight_grads",
    )(x, c, *flat)


def piece(tokens, cotangent, expert_ids, route_gates, gate_proj, up_proj, down_proj):
    groups = lax.axis_size("dp")
    mine, features, units = gate_proj.shape
    experts = mine * groups
    rows, width = tokens.shape
    total = rows * groups
    chosen = expert_ids[:, :, None] == jnp.arange(experts, dtype=jnp.int32)
    weight = jnp.sum(jnp.where(chosen, route_gates.astype(F32)[:, :, None], 0.0), axis=1)
    lanes = -experts % 128
    x, c, weights = gather(tokens, cotangent, jnp.pad(weight, ((0, 0), (0, lanes))).astype(BF16))
    weights = lax.dynamic_slice_in_dim(weights, lax.axis_index("dp") * mine, mine, 1).astype(F32)
    weighted, pre_grads, inner = [], [], []
    for e in range(mine):
        g = weights[:, e : e + 1]
        pre_gate = dot(x, gate_proj[e], 1, 0)
        pre_up = dot(x, up_proj[e], 1, 0)
        back = dot(c, down_proj[e], 1, 1)
        s = jax.nn.sigmoid(pre_gate)
        silu = pre_gate * s
        hidden = silu * pre_up
        grad = back * g
        weighted.append((hidden * g).astype(BF16))
        pre_grads.append((grad * pre_up * s * (1.0 + pre_gate * (1.0 - s))).astype(BF16))
        pre_grads.append((grad * silu).astype(BF16))
        inner.append(jnp.sum(hidden * back, axis=1))
    out_part = sum(dot(weighted[e], down_proj[e], 1, 0) for e in range(mine)).astype(BF16)
    in_part = sum(
        dot(pre_grads[2 * e], gate_proj[e], 1, 1) + dot(pre_grads[2 * e + 1], up_proj[e], 1, 1)
        for e in range(mine)
    ).astype(BF16)
    sums = lax.optimization_barrier(scatter(out_part, in_part))
    grad_gate_w, grad_up_w, grad_down = lax.optimization_barrier(
        weight_grads(x, c, weighted, pre_grads)
    )
    inner = lax.psum(jnp.stack(inner, 1), "et").reshape(groups, rows, mine)
    inner = lax.all_to_all(inner, "dp", 0, 0, tiled=True).transpose(1, 0, 2).reshape(rows, experts)
    grad_gates = jnp.sum(jnp.where(chosen, inner[:, None, :], 0.0), axis=2)
    return (sums[0], sums[1], grad_gates, grad_gate_w, grad_up_w, grad_down)


def local(tokens, cotangent, expert_ids, route_gates, gate_proj, up_proj, down_proj):
    rows = tokens.shape[0]
    pieces = max(1, rows * lax.axis_size("dp") // 1024)
    held = (gate_proj, up_proj, down_proj)
    if pieces == 1 or rows % (16 * pieces):
        return piece(tokens, cotangent, expert_ids, route_gates, *held)

    def step(grads, part):
        done = piece(*part, *held)
        return tuple(a + b for a, b in zip(grads, done[3:])), done[:3]

    split = lambda a: a.reshape(pieces, rows // pieces, *a.shape[1:])
    grads, done = lax.scan(
        step,
        tuple(jnp.zeros(a.shape, F32) for a in held),
        tuple(split(a) for a in (tokens, cotangent, expert_ids, route_gates)),
    )
    return tuple(a.reshape(rows, *a.shape[2:]) for a in done) + grads


def solution(mesh):
    in_specs = (
        P("dp", "et"),
        P("dp", "et"),
        P("dp", None),
        P("dp", None),
        P("dp", None, "et"),
        P("dp", None, "et"),
        P("dp", "et", None),
    )
    out_specs = (
        P("dp", "et"),
        P("dp", "et"),
        P("dp", None),
        P("dp", None, "et"),
        P("dp", None, "et"),
        P("dp", "et", None),
    )
    return jax.shard_map(local, mesh=mesh, in_specs=in_specs, out_specs=out_specs, check_vma=False)
```
